512 devices in a mesh: grp: 8 (over x, core), seq: 64 (over z, y).
Axes of the slice: x: 4, y: 8, z: 8, core: 2. Of those that a mesh axis runs over, the one named last changes fastest.
Arguments:
- llm_grad: bfloat16 [16384, 8192], P('seq', 'grp'), may hold values from -6 to 6
- image_grid: int32 [4096, 2], replicated, may hold values from 1 to 3, as said below
- image_owner: int32 [4096], replicated, may hold values from 0 to 63, as said below
- row_start: int32 [4096], replicated, may hold values from 0 to 255, as said below
- merger_pre: bfloat16 [192, 64, 2560], P(None, 'seq', 'grp'), may hold values from -6 to 6
- vit_out: bfloat16 [768, 64, 1280], P(None, 'seq'), may hold values from -6 to 6
- vit_pre: bfloat16 [768, 64, 2560], P(None, 'seq', 'grp'), may hold values from -6 to 6
- ln_gain: float32 [1280], replicated, may hold values from 0.25 to 1.75
- merger_out_w: bfloat16 [8192, 2560], P('seq', 'grp'), may hold values from -0.0625 to 0.0625
- merger_in_w: bfloat16 [2560, 5120], P('grp', 'seq'), may hold values from -0.125 to 0.125
- vit_fc2_w: bfloat16 [1280, 2560], P('seq', 'grp'), may hold values from -0.15625 to 0.15625
Outputs:
- patch_grad: bfloat16 [768, 64, 1280], P('grp', 'seq')
- fc1_grad: bfloat16 [768, 64, 2560], P(None, 'seq', 'grp')
- fc2_w_grad: float32 [1280, 2560], P('seq', 'grp')
The draws below stay inside these ranges and needn't reach their ends.
Inputs may be any that keep to these rules, and one draw needn't show every extreme that they name: `image_grid`: height times width is 1 to 3; the first image of every shard is 1 by 3; the last image of shard 0 is 1 by 1. `image_owner`: the 64 images of one shard have 64 different owners. An image's rows row_start to row_start + t - 1 lie inside its shard and meet no other image's rows; a shard's images follow the order of k; the last image of every shard ends at the shard's last row; the first image of shard 0 starts at row 0.
All inputs are finite; a program needn't handle non-finite values.
Results may differ from the reference program's by a relative error of at most 0.02.
Values may be sent and summed in bfloat16 or wider, within the bound.
No kernel may reach another device: no remote copies, remote signals or barrier semaphores. Data moves between devices by JAX's collectives and lax.ppermute only.
A program may use at most 64 MiB of HBM per device.

```python
import jax
import jax.numpy as jnp
from jax import lax

D_LLM = 8192
VIT = 1280
HID = 2560
VHID = 2560
SLOT = 3
SEQ_TOK = 256
MERGE_IN = 5120
IMAGES = 4096
MROWS = 192
PSLOT = 768
LLM_TOK = 16384
N_GRP = 8
N_SEQ = 64


def image_layout(key):
    shape_ids = jax.random.randint(jax.random.fold_in(key, 101), (N_SEQ, N_SEQ), 0, 5)
    shape_ids = shape_ids.at[:, 0].set(3)
    shape_ids = shape_ids.at[0, N_SEQ - 1].set(0)
    heights = jnp.array([1, 1, 2, 1, 3], jnp.int32)[shape_ids]
    widths = jnp.array([1, 2, 1, 3, 1], jnp.int32)[shape_ids]
    owner_keys = jax.random.split(jax.random.fold_in(key, 202), N_SEQ)
    owners = jax.vmap(lambda one_key: jax.random.permutation(one_key, N_SEQ))(owner_keys).astype(jnp.int32)
    most_gap = (SEQ_TOK - SLOT * N_SEQ) // N_SEQ
    gap_rows = jax.random.randint(jax.random.fold_in(key, 303), (N_SEQ, N_SEQ), 0, most_gap + 1)
    gap_rows = gap_rows.at[0, 0].set(0)
    token_counts = heights * widths
    span_rows = gap_rows + token_counts
    starts = jnp.cumsum(span_rows, axis=1) - token_counts
    starts = starts.at[:, N_SEQ - 1].set(SEQ_TOK - token_counts[:, N_SEQ - 1])
    return (heights, widths, owners, starts.astype(jnp.int32))


def draw_image_grid(key, part):
    heights, widths, owners, starts = image_layout(key)
    return jnp.stack([heights, widths], -1).reshape(IMAGES, 2).astype(jnp.int32)


def draw_image_owner(key, part):
    heights, widths, owners, starts = image_layout(key)
    return owners.reshape(IMAGES)


def draw_row_start(key, part):
    heights, widths, owners, starts = image_layout(key)
    return starts.reshape(IMAGES)


def shard_levels(key, extent, cuts, least, largest):
    gain = 1.0
    for dim, shards_of in cuts:
        steps = jax.random.uniform(jax.random.fold_in(jax.random.fold_in(key, 6), dim), (shards_of,), jnp.float32, least / len(cuts), largest / len(cuts))
        gain = gain * jnp.repeat(jnp.exp(steps), extent[dim] // shards_of).reshape((-1,) + (1,) * (len(extent) - 1 - dim))
    return gain


def gaussian(own_key, shape, spread, reach, cuts=(), kind=jnp.bfloat16):
    entries = jax.random.normal(own_key, shape, jnp.float32) * spread
    if len(cuts) > 0:
        entries = shard_levels(own_key, shape, cuts, -0.22, 0.18) * entries
    return jnp.clip(entries, min=-reach, max=reach).astype(kind)


def setup_inputs(seed: int = 0) -> dict:
    seeds = jax.random.split(jax.random.key(seed), 12)
    return {
        "llm_grad": gaussian(seeds[0], (LLM_TOK, D_LLM), 1.0, 6.0, ((0, 64), (1, 8))),
        "image_grid": draw_image_grid(jax.random.fold_in(seeds[11], 71), 0),
        "image_owner": draw_image_owner(jax.random.fold_in(seeds[11], 71), 0),
        "row_start": draw_row_start(jax.random.fold_in(seeds[11], 71), 0),
        "merger_pre": gaussian(seeds[4], (MROWS, N_SEQ, HID), 1.0, 6.0, ((1, 64), (2, 8))),
        "vit_out": gaussian(seeds[5], (PSLOT, N_SEQ, VIT), 1.0, 6.0, ((1, 64),)),
        "vit_pre": gaussian(seeds[6], (PSLOT, N_SEQ, VHID), 1.0, 6.0, ((1, 64), (2, 8))),
        "ln_gain": jnp.clip(1.0 + 0.15 * jax.random.normal(seeds[7], (VIT,), jnp.float32), 0.25, 1.75),
        "merger_out_w": gaussian(seeds[8], (D_LLM, HID), D_LLM ** -0.5, 0.0625, ((0, 64), (1, 8))),
        "merger_in_w": gaussian(seeds[9], (HID, MERGE_IN), HID ** -0.5, 0.125, ((0, 8), (1, 64))),
        "vit_fc2_w": gaussian(seeds[10], (VIT, VHID), VIT ** -0.5, 0.15625, ((0, 64), (1, 8))),
    }


def gelu_slope(values):
    return 0.5 * (1.0 + lax.erf(values * 0.7071067811865476)) + values * jnp.exp(-0.5 * values * values) * 0.3989422804014327

def patch_table(widths, counts, slots):
    places = jnp.arange(4 * slots, dtype=jnp.int32)
    merged = places // 4
    corner = places % 4
    row_in = merged[None, :] // widths[:, None]
    col_in = merged[None, :] % widths[:, None]
    target = (2 * row_in + corner[None, :] // 2) * (2 * widths[:, None]) + 2 * col_in + corner[None, :] % 2
    usable = merged[None, :] < counts[:, None]
    return ((target[:, None, :] == places[None, :, None]) & usable[:, None, :]).astype(jnp.float32)

def norm_backward(upstream, inputs, scales):
    average = lax.optimization_barrier(jnp.mean(inputs, -1, keepdims=True))
    centred = inputs - average
    inverse_std = lax.rsqrt(lax.optimization_barrier(jnp.mean(centred * centred, -1, keepdims=True)) + 1e-06)
    normed = centred * inverse_std
    scaled = upstream * scales
    return inverse_std * (scaled - lax.optimization_barrier(jnp.mean(scaled, -1, keepdims=True)) - normed * lax.optimization_barrier(jnp.mean(scaled * normed, -1, keepdims=True)))

def reference(llm_grad, image_grid, image_owner, row_start, merger_pre, vit_out, vit_pre, ln_gain, merger_out_w, merger_in_w, vit_fc2_w):
    grids = image_grid.reshape(N_SEQ, N_SEQ, 2)
    counts = grids[:, :, 0] * grids[:, :, 1]
    widths = grids[:, :, 1]
    owners = image_owner.reshape(N_SEQ, N_SEQ)
    starts = row_start.reshape(N_SEQ, N_SEQ)
    block_width = HID // N_GRP
    sources = jnp.arange(N_SEQ, dtype=jnp.int32)
    within = jnp.arange(SLOT, dtype=jnp.int32)
    in_blocks = merger_in_w.reshape(N_GRP, block_width, MERGE_IN).astype(jnp.float32)

    def one_owner(weight_grad, owner_id):
        chosen = (owners == owner_id).astype(jnp.int32)
        own_counts = lax.optimization_barrier(jnp.sum(chosen * counts, 1))
        own_widths = lax.optimization_barrier(jnp.sum(chosen * widths, 1))
        own_starts = lax.optimization_barrier(jnp.sum(chosen * starts, 1))
        indices = sources[:, None] * SEQ_TOK + jnp.minimum(own_starts[:, None] + within[None, :], SEQ_TOK - 1)
        usable = within[None, :] < own_counts[:, None]
        picked = jnp.take(llm_grad, indices.reshape(-1).astype(jnp.int32), axis=0)
        returned = jnp.where(usable.reshape(-1, 1), picked, jnp.zeros_like(picked))
        hidden_grad = jnp.dot(returned, merger_out_w, preferred_element_type=jnp.float32).astype(jnp.bfloat16)
        pre_act = merger_pre[:, owner_id, :].astype(jnp.float32)
        pre_grad = (gelu_slope(pre_act) * hidden_grad.astype(jnp.float32)).astype(jnp.bfloat16)
        partial_sums = jnp.einsum('rgh,ghc->grc', pre_grad.astype(jnp.float32).reshape(MROWS, N_GRP, block_width), in_blocks)
        rounded = lax.optimization_barrier(partial_sums.astype(jnp.bfloat16))
        merged_grad = lax.optimization_barrier(jnp.sum(rounded.astype(jnp.float32), 0))
        table = patch_table(own_widths, own_counts, SLOT)
        patch_in = jnp.einsum('spq,sqc->spc', table, merged_grad.reshape(N_SEQ, 4 * SLOT, VIT), precision=lax.Precision.HIGHEST).reshape(PSLOT, VIT)
        patch_grad = norm_backward(patch_in, vit_out[:, owner_id, :].astype(jnp.float32), ln_gain).astype(jnp.bfloat16)
        fc_in = vit_pre[:, owner_id, :].astype(jnp.float32)
        sigmoid_q = jax.nn.sigmoid(1.702 * fc_in)
        activation = (fc_in * sigmoid_q).astype(jnp.bfloat16)
        act_grad = jnp.dot(patch_grad, vit_fc2_w, preferred_element_type=jnp.float32)
        fc1_grad = ((sigmoid_q + 1.702 * fc_in * sigmoid_q * (1.0 - sigmoid_q)) * act_grad).astype(jnp.bfloat16)
        weight_grad = weight_grad + lax.dot_general(patch_grad, activation, (((0,), (0,)), ((), ())), preferred_element_type=jnp.float32)
        return (weight_grad, (patch_grad, fc1_grad))
    weight_grad, stacked = lax.scan(one_owner, jnp.zeros((VIT, VHID), jnp.float32), sources)
    return (jnp.transpose(stacked[0], (1, 0, 2)), jnp.transpose(stacked[1], (1, 0, 2)), weight_grad)
```

```python
import jax
import jax.numpy as jnp
from jax import lax
from jax.experimental import pallas as pl
from jax.experimental.pallas import tpu as pltpu
from jax.sharding import Mesh
from jax.sharding import PartitionSpec as P

SLOT = 3
SEQ = ("z", "y")
GRP = ("gx", "gc")
BF16 = jnp.bfloat16
F32 = jnp.float32
PARAMS = pltpu.CompilerParams(vmem_limit_bytes=48 * 1024 * 1024)


def whole(memory=pltpu.VMEM):
    return pl.BlockSpec(memory_space=memory)


def shifted(value, axis, step):
    size = lax.axis_size(axis)
    return lax.ppermute(value, axis, [(i, (i + step) % size) for i in range(size)])


def copy_for_each(value, axis):
    copies = jnp.broadcast_to(value, (lax.axis_size(axis), *value.shape))
    return lax.all_to_all(copies, axis, split_axis=0, concat_axis=0, tiled=True)


def gelu_slope(values):
    return (
        0.5 * (1.0 + lax.erf(values * 0.7071067811865476))
        + values * jnp.exp(-0.5 * values * values) * 0.3989422804014327
    )


def hidden_kernel(order, *refs):
    pieces, (weight, out, sums) = refs[:10], refs[10:]
    w = weight[...]
    for half in range(2):
        near = pieces[5 * half : 5 * half + 5]
        for place in range(3):
            sums[order[4 * half + place]] = jnp.dot(near[place][...], w, preferred_element_type=F32)
        last = jnp.concatenate([near[3][...], near[4][...]], axis=0)
        sums[order[4 * half + 3]] = jnp.dot(last, w, preferred_element_type=F32)
    row = lax.broadcasted_iota(jnp.int32, (192, 192), 0)
    col = lax.broadcasted_iota(jnp.int32, (192, 192), 1)
    wanted = (row // 3 % 8) * 24 + (row // 24) * 3 + row % 3
    turn = jnp.where(wanted == col, 1.0, 0.0).astype(BF16)
    for part in range(8):
        block = sums[:, part * 24 : (part + 1) * 24, :].reshape(192, -1).astype(BF16)
        turned = jnp.dot(turn, block, preferred_element_type=F32)
        out[part * 8 : (part + 1) * 8] = turned.reshape(8, 24, -1).astype(BF16)


def hidden_products(order, pieces, weight):
    width = weight.shape[1]
    return pl.pallas_call(
        hidden_kernel,
        out_shape=jax.ShapeDtypeStruct((64, 24, width), BF16),
        in_specs=[whole(pltpu.SMEM)] + [whole()] * 11,
        out_specs=whole(),
        scratch_shapes=[pltpu.VMEM((8, 192, width), F32)],
        compiler_params=PARAMS,
    )(order, *pieces, weight)


def merged_kernel(core, arrived, slope, blocks, own, other, table):
    for s in range(64):
        table[s * 80 : (s + 1) * 80, :] = blocks[s, 0:80, :]
    total = arrived[0:8].astype(F32)
    for k in range(1, 8):
        total = total + arrived[8 * k : 8 * k + 8].astype(F32)
    hidden = total.reshape(192, -1).astype(BF16).astype(F32)
    grad = (slope[...] * hidden).astype(BF16)
    first = core[0] == 0
    mine = jnp.where(first, grad[:96], grad[96:])
    yours = jnp.where(first, grad[96:], grad[:96])
    dims = (((1,), (1,)), ((), ()))
    for part in range(4):
        w = table[part * 1280 : (part + 1) * 1280, :]
        own[part] = lax.dot_general(mine, w, dims, preferred_element_type=F32).astype(BF16)
        other[part] = lax.dot_general(yours, w, dims, preferred_element_type=F32).astype(BF16)


def merged_products(core, arrived, slope, blocks):
    half = jax.ShapeDtypeStruct((4, 96, 1280), BF16)
    return pl.pallas_call(
        merged_kernel,
        out_shape=(half, half),
        in_specs=[whole(pltpu.SMEM)] + [whole()] * 3,
        out_specs=(whole(), whole()),
        scratch_shapes=[pltpu.VMEM((5120, 320), BF16)],
        compiler_params=PARAMS,
    )(core, arrived, slope, blocks)


def norm_kernel(parts, inputs, gain, out):
    upstream = parts[0].astype(F32)
    for k in range(1, 4):
        upstream = upstream + parts[k].astype(F32)
    x = inputs[...].astype(F32)
    centred = x - jnp.mean(x, -1, keepdims=True)
    inverse_std = lax.rsqrt(jnp.mean(centred * centred, -1, keepdims=True) + 1e-06)
    normed = centred * inverse_std
    scaled = upstream * gain[...]
    out[...] = (
        inverse_std
        * (
            scaled
            - jnp.mean(scaled, -1, keepdims=True)
            - normed * jnp.mean(scaled * normed, -1, keepdims=True)
        )
    ).astype(BF16)


def norm_backward(parts, inputs, gain):
    return pl.pallas_call(
        norm_kernel,
        out_shape=jax.ShapeDtypeStruct((96, 1280), BF16),
        in_specs=[whole()] * 3,
        out_specs=whole(),
        compiler_params=PARAMS,
    )(parts, inputs, gain)


def on_device(
    llm_grad,
    image_grid,
    image_owner,
    row_start,
    merger_pre,
    vit_out,
    vit_pre,
    ln_gain,
    merger_out_w,
    merger_in_w,
    vit_fc2_w,
):
    x = lax.axis_index("gx")
    core = lax.axis_index("gc")
    own_index = lax.axis_index(SEQ)
    bundle = jnp.concatenate(
        [merger_in_w.T, vit_fc2_w, jnp.zeros((4, vit_fc2_w.shape[1]), BF16)], axis=0
    )
    bundles = lax.all_gather(bundle, SEQ, axis=0)

    grids = image_grid.reshape(64, 64, 2)
    counts = grids[:, :, 0] * grids[:, :, 1]
    widths = grids[:, :, 1]
    owners = image_owner.reshape(64, 64)
    starts = row_start.reshape(64, 64)
    peers = jnp.arange(64, dtype=jnp.int32)
    my_owners = lax.dynamic_index_in_dim(owners, own_index, 0, keepdims=False)
    my_counts = lax.dynamic_index_in_dim(counts, own_index, 0, keepdims=False)
    my_starts = lax.dynamic_index_in_dim(starts, own_index, 0, keepdims=False)
    targets = (my_owners[None, :] == peers[:, None]).astype(jnp.int32)
    send_counts = jnp.sum(targets * my_counts[None, :], 1)
    send_starts = jnp.sum(targets * my_starts[None, :], 1)
    within = jnp.arange(SLOT, dtype=jnp.int32)
    wanted = jnp.where(
        within[None, :] < send_counts[:, None], send_starts[:, None] + within[None, :], -1
    ).reshape(-1)
    pick = (wanted[:, None] == jnp.arange(llm_grad.shape[0], dtype=jnp.int32)[None, :]).astype(BF16)
    rows = jnp.dot(pick, llm_grad, preferred_element_type=F32).astype(BF16)

    turned = lax.ppermute(
        rows, (*GRP, "z"), [(g * 8 + z, z * 8 + g) for g in range(8) for z in range(8)]
    )
    out_w = copy_for_each(merger_out_w, "y").reshape(-1, merger_out_w.shape[1])
    left = shifted(turned, "gx", 1)
    right = shifted(turned, "gx", -1)
    far_a = shifted(left[:96], "gx", 1)
    far_b = shifted(right[96:], "gx", -1)
    near = [turned, left, right, far_a, far_b]
    pieces = near + [shifted(piece, "gc", 1) for piece in near]
    order = jnp.stack(
        [
            2 * ((x + step) % 4) + (core + flip) % 2
            for flip in (0, 1)
            for step in (0, 3, 1, 2)
        ]
    ).astype(jnp.int32)
    partial = hidden_products(order, pieces, out_w)
    arrived = lax.all_to_all(partial, SEQ, split_axis=0, concat_axis=0, tiled=True)

    pre_act = (
        merger_pre[:, 0, :].reshape(8, 8, SLOT, -1).transpose(1, 0, 2, 3).reshape(192, -1)
    )
    slope = gelu_slope(pre_act.astype(F32))
    own, other = merged_products(core.reshape(1), arrived, slope, bundles)
    swapped = shifted(other, "gc", 1)
    pair = (own.astype(F32) + swapped.astype(F32)).astype(BF16)
    parts = lax.all_to_all(pair, "gx", split_axis=0, concat_axis=0, tiled=True)

    received = (owners == own_index).astype(jnp.int32)
    recv_counts = jnp.sum(received * counts, 1)
    recv_widths = jnp.sum(received * widths, 1)
    j = jnp.arange(SLOT, dtype=jnp.int32)[None, :]
    w = recv_widths[:, None]
    base = peers[:, None] * (4 * SLOT) + (2 * (j // w)) * (2 * w) + 2 * (j % w)
    valid = j < recv_counts[:, None]
    component = jnp.arange(4, dtype=jnp.int32)[:, None, None]
    slots = base[None] + (component // 2) * (2 * w[None]) + component % 2
    slots = jnp.where(valid[None], slots, -1)
    slots = slots.reshape(4, 8, 8, SLOT).transpose(0, 2, 1, 3).reshape(4, 2, 96)
    slots = slots.transpose(1, 0, 2)
    own_slots = lax.dynamic_index_in_dim(slots, core, 0, keepdims=False)
    other_slots = lax.dynamic_index_in_dim(slots, 1 - core, 0, keepdims=False)
    places = jnp.arange(768, dtype=jnp.int32)
    mine = lax.dynamic_index_in_dim(own_slots, x, 0, keepdims=False)
    take_own = (mine[:, None] == places[None, :]).astype(BF16)
    norm_in = jnp.dot(take_own, vit_out[:, 0, :], preferred_element_type=F32).astype(BF16)
    all_slots = jnp.concatenate([own_slots.reshape(-1), other_slots.reshape(-1)])
    take_all = (all_slots[:, None] == places[None, :]).astype(BF16)
    fc_in = jnp.dot(take_all, vit_pre[:, 0, :], preferred_element_type=F32)
    sigmoid_q = jax.nn.sigmoid(1.702 * fc_in)
    activation = (fc_in * sigmoid_q).astype(BF16)
    fc_slope = sigmoid_q + 1.702 * fc_in * sigmoid_q * (1.0 - sigmoid_q)

    grad = norm_backward(parts, norm_in, ln_gain.reshape(1, -1))
    near_grad = lax.all_gather(grad, "gx", axis=0, tiled=True)
    far_grad = shifted(near_grad, "gc", 1)
    by_row = (((0,), (0,)), ((), ()))
    weight_part = lax.dot_general(
        near_grad, activation[:384], by_row, preferred_element_type=F32
    ) + lax.dot_general(far_grad, activation[384:], by_row, preferred_element_type=F32)
    sent = weight_part.astype(BF16).reshape(64, 20, -1)
    weight_grad = (
        lax.all_to_all(sent, SEQ, split_axis=0, concat_axis=0, tiled=True).astype(F32).sum(axis=0)
    )

    grads = jnp.concatenate([near_grad, far_grad], axis=0)
    fc2 = bundles[:, 80:100].reshape(1280, -1)
    act_grad = jnp.dot(grads, fc2, preferred_element_type=F32)
    fc1_rows = (fc_slope * act_grad).astype(BF16)
    fc1_grad = jnp.dot(take_all.T, fc1_rows, preferred_element_type=F32).astype(BF16)
    g = lax.axis_index(GRP)
    own_places = g * 96 + jnp.arange(96, dtype=jnp.int32)
    put_own = (own_places[:, None] == all_slots[None, :]).astype(BF16)
    own_rows = jnp.dot(put_own, grads, preferred_element_type=F32).astype(BF16)
    return (
        own_rows.reshape(96, 1, -1),
        fc1_grad.reshape(768, 1, -1),
        weight_grad,
    )


def solution(mesh):
    finer = Mesh(mesh.devices.reshape(4, 2, 8, 8), ("gx", "gc", "z", "y"))
    in_specs = (
        P(SEQ, GRP),
        P(),
        P(),
        P(),
        P(None, SEQ, GRP),
        P(None, SEQ, None),
        P(None, SEQ, GRP),
        P(),
        P(SEQ, GRP),
        P(GRP, SEQ),
        P(SEQ, GRP),
    )
    out_specs = (P(GRP, SEQ, None), P(None, SEQ, GRP), P(SEQ, GRP))
    return jax.shard_map(
        on_device, mesh=finer, in_specs=in_specs, out_specs=out_specs, check_vma=False
    )
```

```python
import jax
import jax.numpy as jnp
from jax import lax
from jax.experimental import pallas as pl
from jax.experimental.pallas import tpu as pltpu
from jax.sharding import Mesh
from jax.sharding import PartitionSpec as P

SLOT = 3
SEQ = ("z", "y")
GRP = ("gx", "gc")
BF16 = jnp.bfloat16
F32 = jnp.float32
PARAMS = pltpu.CompilerParams(vmem_limit_bytes=48 * 1024 * 1024)


def whole(memory=pltpu.VMEM):
    return pl.BlockSpec(memory_space=memory)


def shifted(value, axis, step):
    size = lax.axis_size(axis)
    return lax.ppermute(value, axis, [(i, (i + step) % size) for i in range(size)])


def gelu_slope(values):
    return (
        0.5 * (1.0 + lax.erf(values * 0.7071067811865476))
        + values * jnp.exp(-0.5 * values * values) * 0.3989422804014327
    )


def hidden_kernel(order, *refs):
    pieces, (near, far, out, sums, table) = refs[:5], refs[5:]
    last = jnp.concatenate([pieces[3][...], pieces[4][...]], axis=0)
    for core, weight in enumerate((near, far)):
        for k in range(8):
            table[k * 128 : (k + 1) * 128, :] = weight[k, 0:128, :]
        w = table[...]
        for place in range(4):
            rows = pieces[place][...] if place < 3 else last
            sums[order[place] + 4 * core] = jnp.dot(rows, w, preferred_element_type=F32)
    row = lax.broadcasted_iota(jnp.int32, (192, 192), 0)
    col = lax.broadcasted_iota(jnp.int32, (192, 192), 1)
    wanted = (row // 3 % 8) * 24 + (row // 24) * 3 + row % 3
    turn = jnp.where(wanted == col, 1.0, 0.0).astype(BF16)
    for part in range(8):
        block = sums[:, part * 24 : (part + 1) * 24, :].reshape(192, -1).astype(BF16)
        turned = jnp.dot(turn, block, preferred_element_type=F32)
        out[part * 8 : (part + 1) * 8] = turned.reshape(8, 24, -1).astype(BF16)


def hidden_products(order, pieces, near, far):
    width = near.shape[2]
    return pl.pallas_call(
        hidden_kernel,
        out_shape=jax.ShapeDtypeStruct((64, 24, width), BF16),
        in_specs=[whole(pltpu.SMEM)] + [whole()] * 7,
        out_specs=whole(),
        scratch_shapes=[pltpu.VMEM((8, 192, width), F32), pltpu.VMEM((1024, width), BF16)],
        compiler_params=PARAMS,
    )(order, *pieces, near, far)


def sum_kernel(arrived, keep, send):
    total = arrived[0:8].astype(F32)
    for k in range(1, 8):
        total = total + arrived[8 * k : 8 * k + 8].astype(F32)
    hidden = total.reshape(192, -1).astype(BF16)
    row = lax.broadcasted_iota(jnp.int32, (96, 192), 0)
    col = lax.broadcasted_iota(jnp.int32, (96, 192), 1)
    first = row // 12 * 24 + row % 12
    for half, out in enumerate((keep, send)):
        pick = jnp.where(first + 12 * half == col, 1.0, 0.0).astype(BF16)
        out[...] = jnp.dot(pick, hidden, preferred_element_type=F32).astype(BF16)


def hidden_sums(arrived):
    half = jax.ShapeDtypeStruct((96, arrived.shape[2]), BF16)
    return pl.pallas_call(
        sum_kernel,
        out_shape=(half, half),
        in_specs=[whole()],
        out_specs=(whole(), whole()),
        compiler_params=PARAMS,
    )(arrived)


def merged_kernel(kept, received, slope, table, own, other):
    hidden = jnp.concatenate([kept[...], received[...]], axis=0).astype(F32)
    grad = (slope[...] * hidden).astype(BF16)
    dims = (((1,), (1,)), ((), ()))
    for part in range(4):
        w = table[part * 1280 : (part + 1) * 1280, :]
        both = lax.dot_general(grad, w, dims, preferred_element_type=F32).astype(BF16)
        own[part] = both[:96]
        other[part] = both[96:]


def merged_products(kept, received, slope, table):
    half = jax.ShapeDtypeStruct((4, 96, 1280), BF16)
    return pl.pallas_call(
        merged_kernel,
        out_shape=(half, half),
        in_specs=[whole()] * 4,
        out_specs=(whole(), whole()),
        compiler_params=PARAMS,
    )(kept, received, slope, table)


def norm_kernel(parts, inputs, gain, out):
    upstream = parts[0].astype(F32)
    for k in range(1, 4):
        upstream = upstream + parts[k].astype(F32)
    x = inputs[...].astype(F32)
    centred = x - jnp.mean(x, -1, keepdims=True)
    inverse_std = lax.rsqrt(jnp.mean(centred * centred, -1, keepdims=True) + 1e-06)
    normed = centred * inverse_std
    scaled = upstream * gain[...]
    out[...] = (
        inverse_std
        * (
            scaled
            - jnp.mean(scaled, -1, keepdims=True)
            - normed * jnp.mean(scaled * normed, -1, keepdims=True)
        )
    ).astype(BF16)


def norm_backward(parts, inputs, gain):
    return pl.pallas_call(
        norm_kernel,
        out_shape=jax.ShapeDtypeStruct((96, 1280), BF16),
        in_specs=[whole()] * 3,
        out_specs=whole(),
        compiler_params=PARAMS,
    )(parts, inputs, gain)


def weight_kernel(near, far, activation, out, total, turned, packed):
    dims = (((0,), (0,)), ((), ()))
    total[:, 256:384] = jnp.zeros((1280, 128), F32)
    total[:, 0:320] = lax.dot_general(
        near[...], activation[0:384, :], dims, preferred_element_type=F32
    ) + lax.dot_general(far[...], activation[384:768, :], dims, preferred_element_type=F32)
    turned[...] = pltpu.roll(total[:, 256:384], 64, 1)
    for s in range(64):
        row = s * 20
        packed[s, 0:20, :] = total[row : row + 20, 0:128]
        packed[s, 20:40, :] = total[row : row + 20, 128:256]
        packed[s, 40:50, :] = total[row : row + 10, 256:384] + turned[row + 10 : row + 20, :]
        packed[s, 50:56, :] = jnp.zeros((6, 128), F32)
    out[...] = packed[...].astype(BF16)


def weight_products(near, far, activation):
    return pl.pallas_call(
        weight_kernel,
        out_shape=jax.ShapeDtypeStruct((64, 56, 128), BF16),
        in_specs=[whole()] * 3,
        out_specs=whole(),
        scratch_shapes=[
            pltpu.VMEM((1280, 384), F32),
            pltpu.VMEM((1280, 128), F32),
            pltpu.VMEM((64, 56, 128), F32),
        ],
        compiler_params=PARAMS,
    )(near, far, activation)


def unpack_kernel(arrived, out, total, turned):
    total[...] = jnp.sum(arrived[...].astype(F32), axis=0)
    turned[...] = pltpu.roll(total[...], 64, 1)
    out[:, 0:128] = total[0:20, :]
    out[:, 128:256] = total[20:40, :]
    out[0:10, 256:320] = total[40:50, 0:64]
    out[10:20, 256:320] = turned[40:50, 0:64]


def weight_sums(arrived):
    return pl.pallas_call(
        unpack_kernel,
        out_shape=jax.ShapeDtypeStruct((20, 320), F32),
        in_specs=[whole()],
        out_specs=whole(),
        scratch_shapes=[pltpu.VMEM((56, 128), F32), pltpu.VMEM((56, 128), F32)],
        compiler_params=PARAMS,
    )(arrived)


def on_device(
    llm_grad,
    image_grid,
    image_owner,
    row_start,
    merger_pre,
    vit_out,
    vit_pre,
    ln_gain,
    merger_out_w,
    merger_in_w,
    vit_fc2_w,
):
    x = lax.axis_index("gx")
    core = lax.axis_index("gc")
    own_index = lax.axis_index(SEQ)
    peers = jnp.arange(64, dtype=jnp.int32)
    my_owners = lax.dynamic_slice_in_dim(image_owner, own_index * 64, 64)
    my_starts = lax.dynamic_slice_in_dim(row_start, own_index * 64, 64)
    my_grids = lax.dynamic_slice_in_dim(image_grid, own_index * 64, 64)
    my_counts = my_grids[:, 0] * my_grids[:, 1]
    targets = (my_owners[None, :] == peers[:, None]).astype(jnp.int32)
    send_counts = jnp.sum(targets * my_counts[None, :], 1)
    send_starts = jnp.sum(targets * my_starts[None, :], 1)
    within = jnp.arange(SLOT, dtype=jnp.int32)
    wanted = jnp.where(
        within[None, :] < send_counts[:, None], send_starts[:, None] + within[None, :], -1
    ).reshape(-1)
    pick = (wanted[:, None] == jnp.arange(llm_grad.shape[0], dtype=jnp.int32)[None, :]).astype(BF16)
    rows = jnp.dot(pick, llm_grad, preferred_element_type=F32).astype(BF16)

    fc2_rows = jnp.pad(vit_fc2_w, ((0, 12), (0, 0)))
    rows, fc2_rows = lax.optimization_barrier((rows, fc2_rows))
    along_y = lax.all_gather(jnp.concatenate([merger_out_w, fc2_rows], axis=0), "y", axis=0)
    turned = lax.ppermute(
        rows, (*GRP, "z"), [(g * 8 + z, z * 8 + g) for g in range(8) for z in range(8)]
    )
    turned, along_y = lax.optimization_barrier((turned, along_y))
    across = shifted(along_y, "gc", 1)
    left = shifted(turned, "gx", 1)
    right = shifted(turned, "gx", -1)
    far_a = shifted(left[:96], "gx", 1)
    far_b = shifted(right[96:], "gx", -1)
    pieces = [turned, left, right, far_a, far_b]
    order = jnp.stack([(x + step) % 4 for step in (0, 3, 1, 2)]).astype(jnp.int32)
    partial = hidden_products(order, pieces, along_y, across)
    partial, merger_pre, image_owner, image_grid, vit_pre, vit_out = lax.optimization_barrier(
        (partial, merger_pre, image_owner, image_grid, vit_pre, vit_out)
    )
    arrived = lax.all_to_all(partial, SEQ, split_axis=0, concat_axis=0, tiled=True)

    pre_act = merger_pre[:, 0, :].reshape(4, 2, 8, SLOT, -1).transpose(1, 2, 0, 3, 4)
    pre_act = pre_act.reshape(2, 96, -1)
    pre_act = jnp.where(core == 0, pre_act, pre_act[::-1]).reshape(192, -1)
    slope = gelu_slope(pre_act.astype(F32))
    table = lax.all_gather(merger_in_w.T, SEQ, axis=0, tiled=True)
    fc2_y = along_y[:, 128:, :].reshape(256, -1)
    fc2 = lax.all_gather(fc2_y, "z", axis=0, tiled=True)
    kept, passed = hidden_sums(arrived)
    own, other = merged_products(kept, shifted(passed, "gc", 1), slope, table)
    swapped = shifted(other, "gc", 1)
    pair = (own.astype(F32) + swapped.astype(F32)).astype(BF16)
    parts = lax.all_to_all(pair, "gx", split_axis=0, concat_axis=0, tiled=True)

    grids = image_grid.reshape(64, 64, 2)
    counts = grids[:, :, 0] * grids[:, :, 1]
    widths = grids[:, :, 1]
    owners = image_owner.reshape(64, 64)
    received = (owners == own_index).astype(jnp.int32)
    recv_counts = jnp.sum(received * counts, 1)
    recv_widths = jnp.sum(received * widths, 1)
    j = jnp.arange(SLOT, dtype=jnp.int32)[None, :]
    w = recv_widths[:, None]
    base = peers[:, None] * (4 * SLOT) + (2 * (j // w)) * (2 * w) + 2 * (j % w)
    valid = j < recv_counts[:, None]
    component = jnp.arange(4, dtype=jnp.int32)[:, None, None]
    slots = base[None] + (component // 2) * (2 * w[None]) + component % 2
    slots = jnp.where(valid[None], slots, -1)
    slots = slots.reshape(4, 4, 2, 8, SLOT).transpose(2, 0, 3, 1, 4).reshape(2, 4, 96)
    own_slots = lax.dynamic_index_in_dim(slots, core, 0, keepdims=False)
    other_slots = lax.dynamic_index_in_dim(slots, 1 - core, 0, keepdims=False)
    places = jnp.arange(768, dtype=jnp.int32)
    mine = lax.dynamic_index_in_dim(own_slots, x, 0, keepdims=False)
    take_own = (mine[:, None] == places[None, :]).astype(BF16)
    norm_in = jnp.dot(take_own, vit_out[:, 0, :], preferred_element_type=F32).astype(BF16)
    all_slots = jnp.concatenate([own_slots.reshape(-1), other_slots.reshape(-1)])
    take_all = (all_slots[:, None] == places[None, :]).astype(BF16)
    fc_in = jnp.dot(take_all, vit_pre[:, 0, :], preferred_element_type=F32)
    sigmoid_q = jax.nn.sigmoid(1.702 * fc_in)
    activation = (fc_in * sigmoid_q).astype(BF16)
    fc_slope = sigmoid_q + 1.702 * fc_in * sigmoid_q * (1.0 - sigmoid_q)

    grad = norm_backward(parts, norm_in, ln_gain.reshape(1, -1))
    near_grad = lax.all_gather(grad, "gx", axis=0, tiled=True)
    far_grad = shifted(near_grad, "gc", 1)
    sent = weight_products(near_grad, far_grad, activation)
    weight_grad = weight_sums(
        lax.all_to_all(sent, SEQ, split_axis=0, concat_axis=0, tiled=True)
    )

    grads = jnp.concatenate([near_grad, far_grad], axis=0)
    fc2 = fc2.reshape(64, 32, -1)[:, :20].reshape(1280, -1)
    act_grad = jnp.dot(grads, fc2, preferred_element_type=F32)
    fc1_rows = (fc_slope * act_grad).astype(BF16)
    fc1_grad = jnp.dot(take_all.T, fc1_rows, preferred_element_type=F32).astype(BF16)
    g = lax.axis_index(GRP)
    own_places = g * 96 + jnp.arange(96, dtype=jnp.int32)
    put_own = (own_places[:, None] == all_slots[None, :]).astype(BF16)
    own_rows = jnp.dot(put_own, grads, preferred_element_type=F32).astype(BF16)
    return (
        own_rows.reshape(96, 1, -1),
        fc1_grad.reshape(768, 1, -1),
        weight_grad,
    )


def solution(mesh):
    finer = Mesh(mesh.devices.reshape(4, 2, 8, 8), ("gx", "gc", "z", "y"))
    in_specs = (
        P(SEQ, GRP),
        P(),
        P(),
        P(),
        P(None, SEQ, GRP),
        P(None, SEQ, None),
        P(None, SEQ, GRP),
        P(),
        P(SEQ, GRP),
        P(GRP, SEQ),
        P(SEQ, GRP),
    )
    out_specs = (P(GRP, SEQ, None), P(None, SEQ, GRP), P(SEQ, GRP))
    return jax.shard_map(
        on_device, mesh=finer, in_specs=in_specs, out_specs=out_specs, check_vma=False
    )
```

```python
import jax
import jax.numpy as jnp
from jax import lax
from jax.experimental import pallas as pl
from jax.experimental.pallas import tpu as pltpu
from jax.sharding import Mesh
from jax.sharding import PartitionSpec as P

SLOT = 3
SEQ = ("z", "y")
GRP = ("gx", "gc")
BF16 = jnp.bfloat16
F32 = jnp.float32
PARAMS = pltpu.CompilerParams(vmem_limit_bytes=48 * 1024 * 1024)


def whole(memory=pltpu.VMEM):
    return pl.BlockSpec(memory_space=memory)


def shifted(value, axis, step):
    size = lax.axis_size(axis)
    return lax.ppermute(value, axis, [(i, (i + step) % size) for i in range(size)])


def gelu_slope(values):
    return (
        0.5 * (1.0 + lax.erf(values * 0.7071067811865476))
        + values * jnp.exp(-0.5 * values * values) * 0.3989422804014327
    )


def hidden_kernel(order, *refs):
    pieces, (near, far, out, sums, table) = refs[:8], refs[8:]
    table[:, 256:384] = jnp.zeros((1024, 128), BF16)
    for core, weight in enumerate((near, far)):
        for k in range(8):
            table[k * 128 : (k + 1) * 128, 0:320] = weight[k, 0:128, :]
        w = table[...]
        for place in range(4):
            rows = jnp.concatenate([half[...] for half in pieces[2 * place : 2 * place + 2]], axis=0)
            sums[order[place] + 4 * core] = jnp.dot(rows, w, preferred_element_type=F32)
    row = lax.broadcasted_iota(jnp.int32, (192, 192), 0)
    col = lax.broadcasted_iota(jnp.int32, (192, 192), 1)
    wanted = (row // 3 % 8) * 24 + (row // 24) * 3 + row % 3
    turn = jnp.where(wanted == col, 1.0, 0.0).astype(BF16)
    for part in range(8):
        block = sums[:, part * 24 : (part + 1) * 24, :].reshape(192, -1).astype(BF16)
        turned = jnp.dot(turn, block, preferred_element_type=F32)
        last = turned[:, 256:384]
        shifted_last = pltpu.roll(last, 64, 1).reshape(8, 24, 128)
        last = last.reshape(8, 24, 128)
        packed = jnp.concatenate(
            [
                turned[:, 0:128].reshape(8, 24, 128),
                turned[:, 128:256].reshape(8, 24, 128),
                last[:, 0:8] + shifted_last[:, 8:16],
                last[:, 16:24],
            ],
            axis=1,
        )
        out[part * 8 : (part + 1) * 8] = packed.astype(BF16)


def hidden_products(order, pieces, near, far):
    return pl.pallas_call(
        hidden_kernel,
        out_shape=jax.ShapeDtypeStruct((64, 64, 128), BF16),
        in_specs=[whole(pltpu.SMEM)] + [whole()] * 10,
        out_specs=whole(),
        scratch_shapes=[pltpu.VMEM((8, 192, 384), F32), pltpu.VMEM((1024, 384), BF16)],
        compiler_params=PARAMS,
    )(order, *pieces, near, far)


def sum_kernel(arrived, keep, send):
    total = arrived[0:8].astype(F32)
    for k in range(1, 8):
        total = total + arrived[8 * k : 8 * k + 8].astype(F32)
    last = total[:, 48:56]
    second = pltpu.roll(last.reshape(64, 128), 64, 1).reshape(8, 8, 128)
    last = jnp.concatenate([last, second, total[:, 56:64]], axis=1)
    hidden = jnp.concatenate(
        [part.reshape(192, 128) for part in (total[:, 0:24], total[:, 24:48], last)], axis=1
    ).astype(BF16)
    row = lax.broadcasted_iota(jnp.int32, (96, 192), 0)
    col = lax.broadcasted_iota(jnp.int32, (96, 192), 1)
    first = row // 12 * 24 + row % 12
    for half, out in enumerate((keep, send)):
        pick = jnp.where(first + 12 * half == col, 1.0, 0.0).astype(BF16)
        out[...] = jnp.dot(pick, hidden, preferred_element_type=F32)[:, 0:320].astype(BF16)


def hidden_sums(arrived):
    half = jax.ShapeDtypeStruct((96, 320), BF16)
    return pl.pallas_call(
        sum_kernel,
        out_shape=(half, half),
        in_specs=[whole()],
        out_specs=(whole(), whole()),
        compiler_params=PARAMS,
    )(arrived)


def merged_kernel(kept, received, slope, table, own, other):
    hidden = jnp.concatenate([kept[...], received[...]], axis=0).astype(F32)
    grad = (slope[...] * hidden).astype(BF16)
    dims = (((1,), (1,)), ((), ()))
    for part in range(4):
        w = table[part * 1280 : (part + 1) * 1280, :]
        both = lax.dot_general(grad, w, dims, preferred_element_type=F32).astype(BF16)
        own[part] = both[:96]
        other[part] = both[96:]


def merged_products(kept, received, slope, table):
    half = jax.ShapeDtypeStruct((4, 96, 1280), BF16)
    return pl.pallas_call(
        merged_kernel,
        out_shape=(half, half),
        in_specs=[whole()] * 4,
        out_specs=(whole(), whole()),
        compiler_params=PARAMS,
    )(kept, received, slope, table)


def norm_kernel(parts, inputs, gain, out):
    upstream = parts[0].astype(F32)
    for k in range(1, 4):
        upstream = upstream + parts[k].astype(F32)
    x = inputs[...].astype(F32)
    centred = x - jnp.mean(x, -1, keepdims=True)
    inverse_std = lax.rsqrt(jnp.mean(centred * centred, -1, keepdims=True) + 1e-06)
    normed = centred * inverse_std
    scaled = upstream * gain[...]
    out[...] = (
        inverse_std
        * (
            scaled
            - jnp.mean(scaled, -1, keepdims=True)
            - normed * jnp.mean(scaled * normed, -1, keepdims=True)
        )
    ).astype(BF16)


def norm_backward(parts, inputs, gain):
    return pl.pallas_call(
        norm_kernel,
        out_shape=jax.ShapeDtypeStruct((96, 1280), BF16),
        in_specs=[whole()] * 3,
        out_specs=whole(),
        compiler_params=PARAMS,
    )(parts, inputs, gain)


def weight_kernel(near, far, activation, out, total, turned, packed):
    dims = (((0,), (0,)), ((), ()))
    total[:, 256:384] = jnp.zeros((1280, 128), F32)
    total[:, 0:320] = lax.dot_general(
        near[...], activation[0:384, :], dims, preferred_element_type=F32
    ) + lax.dot_general(far[...], activation[384:768, :], dims, preferred_element_type=F32)
    turned[...] = pltpu.roll(total[:, 256:384], 64, 1)
    for s in range(64):
        row = s * 20
        packed[s, 0:20, :] = total[row : row + 20, 0:128]
        packed[s, 20:40, :] = total[row : row + 20, 128:256]
        packed[s, 40:50, :] = total[row : row + 10, 256:384] + turned[row + 10 : row + 20, :]
        packed[s, 50:56, :] = jnp.zeros((6, 128), F32)
    out[...] = packed[...].astype(BF16)


def weight_products(near, far, activation):
    return pl.pallas_call(
        weight_kernel,
        out_shape=jax.ShapeDtypeStruct((64, 56, 128), BF16),
        in_specs=[whole()] * 3,
        out_specs=whole(),
        scratch_shapes=[
            pltpu.VMEM((1280, 384), F32),
            pltpu.VMEM((1280, 128), F32),
            pltpu.VMEM((64, 56, 128), F32),
        ],
        compiler_params=PARAMS,
    )(near, far, activation)


def unpack_kernel(arrived, out, total, turned):
    total[...] = jnp.sum(arrived[...].astype(F32), axis=0)
    turned[...] = pltpu.roll(total[...], 64, 1)
    out[:, 0:128] = total[0:20, :]
    out[:, 128:256] = total[20:40, :]
    out[0:10, 256:320] = total[40:50, 0:64]
    out[10:20, 256:320] = turned[40:50, 0:64]


def weight_sums(arrived):
    return pl.pallas_call(
        unpack_kernel,
        out_shape=jax.ShapeDtypeStruct((20, 320), F32),
        in_specs=[whole()],
        out_specs=whole(),
        scratch_shapes=[pltpu.VMEM((56, 128), F32), pltpu.VMEM((56, 128), F32)],
        compiler_params=PARAMS,
    )(arrived)


def on_device(
    llm_grad,
    image_grid,
    image_owner,
    row_start,
    merger_pre,
    vit_out,
    vit_pre,
    ln_gain,
    merger_out_w,
    merger_in_w,
    vit_fc2_w,
):
    x = lax.axis_index("gx")
    core = lax.axis_index("gc")
    own_index = lax.axis_index(SEQ)
    peers = jnp.arange(64, dtype=jnp.int32)
    my_owners = lax.dynamic_slice_in_dim(image_owner, own_index * 64, 64)
    my_starts = lax.dynamic_slice_in_dim(row_start, own_index * 64, 64)
    my_grids = lax.dynamic_slice_in_dim(image_grid, own_index * 64, 64)
    my_counts = my_grids[:, 0] * my_grids[:, 1]
    targets = (my_owners[None, :] == peers[:, None]).astype(jnp.int32)
    send_counts = jnp.sum(targets * my_counts[None, :], 1)
    send_starts = jnp.sum(targets * my_starts[None, :], 1)
    within = jnp.arange(SLOT, dtype=jnp.int32)
    wanted = jnp.where(
        within[None, :] < send_counts[:, None], send_starts[:, None] + within[None, :], -1
    ).reshape(-1)
    pick = (wanted[:, None] == jnp.arange(llm_grad.shape[0], dtype=jnp.int32)[None, :]).astype(BF16)
    rows = jnp.dot(pick, llm_grad, preferred_element_type=F32).astype(BF16)

    fc2_rows = jnp.pad(vit_fc2_w, ((0, 12), (0, 0)))
    rows, fc2_rows = lax.optimization_barrier((rows, fc2_rows))
    along_y = lax.all_gather(jnp.concatenate([merger_out_w, fc2_rows], axis=0), "y", axis=0)
    turned = lax.ppermute(
        rows, (*GRP, "z"), [(g * 8 + z, z * 8 + g) for g in range(8) for z in range(8)]
    )
    turned, along_y = lax.optimization_barrier((turned, along_y))
    across = shifted(along_y, "gc", 1)
    top, low = turned[:96], turned[96:]
    left_top = shifted(top, "gx", 1)
    right_low = shifted(low, "gx", -1)
    left_low = shifted(low, "gx", 1)
    right_top = shifted(top, "gx", -1)
    far_top = shifted(left_top, "gx", 1)
    far_low = shifted(right_low, "gx", -1)
    pieces = [top, low, left_top, left_low, right_top, right_low, far_top, far_low]
    order = jnp.stack([(x + step) % 4 for step in (0, 3, 1, 2)]).astype(jnp.int32)
    partial = hidden_products(order, pieces, along_y, across)
    partial, merger_pre, image_owner, image_grid, vit_pre, vit_out = lax.optimization_barrier(
        (partial, merger_pre, image_owner, image_grid, vit_pre, vit_out)
    )
    arrived = lax.all_to_all(partial, SEQ, split_axis=0, concat_axis=0, tiled=True)

    pre_act = merger_pre[:, 0, :].reshape(4, 2, 8, SLOT, -1).transpose(1, 2, 0, 3, 4)
    pre_act = pre_act.reshape(2, 96, -1)
    pre_act = jnp.where(core == 0, pre_act, pre_act[::-1]).reshape(192, -1)
    slope = gelu_slope(pre_act.astype(F32))
    table = lax.all_gather(merger_in_w.T, SEQ, axis=0, tiled=True)
    fc2_y = along_y[:, 128:, :].reshape(256, -1)
    arrived, fc2_y = lax.optimization_barrier((arrived, fc2_y))
    fc2 = lax.all_gather(fc2_y, "z", axis=0, tiled=True)
    kept, passed = hidden_sums(arrived)
    own, other = merged_products(kept, shifted(passed, "gc", 1), slope, table)
    pair = (own.astype(F32) + shifted(other, "gc", 1).astype(F32)).astype(BF16)
    parts = lax.all_to_all(pair, "gx", split_axis=0, concat_axis=0, tiled=True)

    grids = image_grid.reshape(64, 64, 2)
    counts = grids[:, :, 0] * grids[:, :, 1]
    widths = grids[:, :, 1]
    owners = image_owner.reshape(64, 64)
    taken = (owners == own_index).astype(jnp.int32)
    recv_counts = jnp.sum(taken * counts, 1)
    recv_widths = jnp.sum(taken * widths, 1)
    j = jnp.arange(SLOT, dtype=jnp.int32)[None, :]
    w = recv_widths[:, None]
    base = peers[:, None] * (4 * SLOT) + (2 * (j // w)) * (2 * w) + 2 * (j % w)
    valid = j < recv_counts[:, None]
    component = jnp.arange(4, dtype=jnp.int32)[:, None, None]
    slots = base[None] + (component // 2) * (2 * w[None]) + component % 2
    slots = jnp.where(valid[None], slots, -1)
    slots = slots.reshape(4, 4, 2, 8, SLOT).transpose(2, 0, 3, 1, 4).reshape(2, 4, 96)
    own_slots = lax.dynamic_index_in_dim(slots, core, 0, keepdims=False)
    other_slots = lax.dynamic_index_in_dim(slots, 1 - core, 0, keepdims=False)
    places = jnp.arange(768, dtype=jnp.int32)
    mine = lax.dynamic_index_in_dim(own_slots, x, 0, keepdims=False)
    take_own = (mine[:, None] == places[None, :]).astype(BF16)
    norm_in = jnp.dot(take_own, vit_out[:, 0, :], preferred_element_type=F32).astype(BF16)
    all_slots = jnp.concatenate([own_slots.reshape(-1), other_slots.reshape(-1)])
    take_all = (all_slots[:, None] == places[None, :]).astype(BF16)
    fc_in = jnp.dot(take_all, vit_pre[:, 0, :], preferred_element_type=F32)
    sigmoid_q = jax.nn.sigmoid(1.702 * fc_in)
    activation = (fc_in * sigmoid_q).astype(BF16)
    fc_slope = sigmoid_q + 1.702 * fc_in * sigmoid_q * (1.0 - sigmoid_q)

    grad = norm_backward(parts, norm_in, ln_gain.reshape(1, -1))
    near_grad = lax.all_gather(grad, "gx", axis=0, tiled=True)
    far_grad = shifted(near_grad, "gc", 1)
    sent = weight_products(near_grad, far_grad, activation)
    weight_grad = weight_sums(
        lax.all_to_all(sent, SEQ, split_axis=0, concat_axis=0, tiled=True)
    )

    grads = jnp.concatenate([near_grad, far_grad], axis=0)
    fc2 = fc2.reshape(64, 32, -1)[:, :20].reshape(1280, -1)
    act_grad = jnp.dot(grads, fc2, preferred_element_type=F32)
    fc1_rows = (fc_slope * act_grad).astype(BF16)
    fc1_grad = jnp.dot(take_all.T, fc1_rows, preferred_element_type=F32).astype(BF16)
    g = lax.axis_index(GRP)
    own_places = g * 96 + jnp.arange(96, dtype=jnp.int32)
    put_own = (own_places[:, None] == all_slots[None, :]).astype(BF16)
    own_rows = jnp.dot(put_own, grads, preferred_element_type=F32).astype(BF16)
    return (
        own_rows.reshape(96, 1, -1),
        fc1_grad.reshape(768, 1, -1),
        weight_grad,
    )


def solution(mesh):
    finer = Mesh(mesh.devices.reshape(4, 2, 8, 8), ("gx", "gc", "z", "y"))
    in_specs = (
        P(SEQ, GRP),
        P(),
        P(),
        P(),
        P(None, SEQ, GRP),
        P(None, SEQ, None),
        P(None, SEQ, GRP),
        P(),
        P(SEQ, GRP),
        P(GRP, SEQ),
        P(SEQ, GRP),
    )
    out_specs = (P(GRP, SEQ, None), P(None, SEQ, GRP), P(SEQ, GRP))
    return jax.shard_map(
        on_device, mesh=finer, in_specs=in_specs, out_specs=out_specs, check_vma=False
    )
```

```python
import jax
import jax.numpy as jnp
from jax import lax
from jax.experimental import pallas as pl
from jax.experimental.pallas import tpu as pltpu
from jax.sharding import Mesh
from jax.sharding import PartitionSpec as P

SLOT = 3
SEQ = ("z", "y")
GRP = ("gx", "gc")
BF16 = jnp.bfloat16
F32 = jnp.float32
PARAMS = pltpu.CompilerParams(vmem_limit_bytes=48 * 1024 * 1024)


def whole(memory=pltpu.VMEM):
    return pl.BlockSpec(memory_space=memory)


def shifted(value, axis, step):
    size = lax.axis_size(axis)
    return lax.ppermute(value, axis, [(i, (i + step) % size) for i in range(size)])


def gelu_slope(values):
    return (
        0.5 * (1.0 + lax.erf(values * 0.7071067811865476))
        + values * jnp.exp(-0.5 * values * values) * 0.3989422804014327
    )


def hidden_kernel(order, *refs):
    pieces, (near, far, out, sums, table) = refs[:8], refs[8:]
    table[:, 256:384] = jnp.zeros((1024, 128), BF16)
    for core, weight in enumerate((near, far)):
        for k in range(8):
            table[k * 128 : (k + 1) * 128, 0:320] = weight[k, 0:128, :]
        w = table[...]
        for place in range(4):
            rows = jnp.concatenate([half[...] for half in pieces[2 * place : 2 * place + 2]], axis=0)
            sums[order[place] + 4 * core] = jnp.dot(rows, w, preferred_element_type=F32)
    row = lax.broadcasted_iota(jnp.int32, (192, 192), 0)
    col = lax.broadcasted_iota(jnp.int32, (192, 192), 1)
    wanted = (row // 3 % 8) * 24 + (row // 24) * 3 + row % 3
    turn = jnp.where(wanted == col, 1.0, 0.0).astype(BF16)
    for part in range(8):
        block = sums[:, part * 24 : (part + 1) * 24, :].reshape(192, -1).astype(BF16)
        turned = jnp.dot(turn, block, preferred_element_type=F32)
        last = turned[:, 256:384]
        shifted_last = pltpu.roll(last, 64, 1).reshape(8, 24, 128)
        last = last.reshape(8, 24, 128)
        packed = jnp.concatenate(
            [
                turned[:, 0:128].reshape(8, 24, 128),
                turned[:, 128:256].reshape(8, 24, 128),
                last[:, 0:8] + shifted_last[:, 8:16],
                last[:, 16:24],
            ],
            axis=1,
        )
        out[part * 8 : (part + 1) * 8] = packed.astype(BF16)


def hidden_products(order, pieces, near, far):
    return pl.pallas_call(
        hidden_kernel,
        out_shape=jax.ShapeDtypeStruct((64, 64, 128), BF16),
        in_specs=[whole(pltpu.SMEM)] + [whole()] * 10,
        out_specs=whole(),
        scratch_shapes=[pltpu.VMEM((8, 192, 384), F32), pltpu.VMEM((1024, 384), BF16)],
        compiler_params=PARAMS,
    )(order, *pieces, near, far)


def sum_kernel(arrived, keep, send):
    total = arrived[0:8].astype(F32)
    for k in range(1, 8):
        total = total + arrived[8 * k : 8 * k + 8].astype(F32)
    last = total[:, 48:56]
    second = pltpu.roll(last.reshape(64, 128), 64, 1).reshape(8, 8, 128)
    last = jnp.concatenate([last, second, total[:, 56:64]], axis=1)
    hidden = jnp.concatenate(
        [part.reshape(192, 128) for part in (total[:, 0:24], total[:, 24:48], last)], axis=1
    ).astype(BF16)
    row = lax.broadcasted_iota(jnp.int32, (96, 192), 0)
    col = lax.broadcasted_iota(jnp.int32, (96, 192), 1)
    first = row // 12 * 24 + row % 12
    for half, out in enumerate((keep, send)):
        pick = jnp.where(first + 12 * half == col, 1.0, 0.0).astype(BF16)
        out[...] = jnp.dot(pick, hidden, preferred_element_type=F32)[:, 0:320].astype(BF16)


def hidden_sums(arrived):
    half = jax.ShapeDtypeStruct((96, 320), BF16)
    return pl.pallas_call(
        sum_kernel,
        out_shape=(half, half),
        in_specs=[whole()],
        out_specs=(whole(), whole()),
        compiler_params=PARAMS,
    )(arrived)


def merged_kernel(grads, table, own, other):
    dims = (((1,), (1,)), ((), ()))
    total = None
    for k in range(4):
        w = table[k * 1280 : (k + 1) * 1280, :]
        part = lax.dot_general(grads[k], w, dims, preferred_element_type=F32)
        total = part if total is None else total + part
    own[...] = total[:96]
    other[...] = total[96:].astype(BF16)


def merged_products(grads, table):
    return pl.pallas_call(
        merged_kernel,
        out_shape=(
            jax.ShapeDtypeStruct((96, 1280), F32),
            jax.ShapeDtypeStruct((96, 1280), BF16),
        ),
        in_specs=[whole()] * 2,
        out_specs=(whole(), whole()),
        compiler_params=PARAMS,
    )(grads, table)


def norm_kernel(own, swapped, inputs, gain, out):
    upstream = own[...] + swapped[...].astype(F32)
    x = inputs[...].astype(F32)
    centred = x - jnp.mean(x, -1, keepdims=True)
    inverse_std = lax.rsqrt(jnp.mean(centred * centred, -1, keepdims=True) + 1e-06)
    normed = centred * inverse_std
    scaled = upstream * gain[...]
    out[...] = (
        inverse_std
        * (
            scaled
            - jnp.mean(scaled, -1, keepdims=True)
            - normed * jnp.mean(scaled * normed, -1, keepdims=True)
        )
    ).astype(BF16)


def norm_backward(own, swapped, inputs, gain):
    return pl.pallas_call(
        norm_kernel,
        out_shape=jax.ShapeDtypeStruct((96, 1280), BF16),
        in_specs=[whole()] * 4,
        out_specs=whole(),
        compiler_params=PARAMS,
    )(own, swapped, inputs, gain)


def weight_kernel(near, far, activation, out, total, turned, packed):
    dims = (((0,), (0,)), ((), ()))
    total[:, 256:384] = jnp.zeros((1280, 128), F32)
    total[:, 0:320] = lax.dot_general(
        near[...], activation[0:384, :], dims, preferred_element_type=F32
    ) + lax.dot_general(far[...], activation[384:768, :], dims, preferred_element_type=F32)
    turned[...] = pltpu.roll(total[:, 256:384], 64, 1)
    for s in range(64):
        row = s * 20
        packed[s, 0:20, :] = total[row : row + 20, 0:128]
        packed[s, 20:40, :] = total[row : row + 20, 128:256]
        packed[s, 40:50, :] = total[row : row + 10, 256:384] + turned[row + 10 : row + 20, :]
        packed[s, 50:56, :] = jnp.zeros((6, 128), F32)
    out[...] = packed[...].astype(BF16)


def weight_products(near, far, activation):
    return pl.pallas_call(
        weight_kernel,
        out_shape=jax.ShapeDtypeStruct((64, 56, 128), BF16),
        in_specs=[whole()] * 3,
        out_specs=whole(),
        scratch_shapes=[
            pltpu.VMEM((1280, 384), F32),
            pltpu.VMEM((1280, 128), F32),
            pltpu.VMEM((64, 56, 128), F32),
        ],
        compiler_params=PARAMS,
    )(near, far, activation)


def unpack_kernel(arrived, out, total, turned):
    total[...] = jnp.sum(arrived[...].astype(F32), axis=0)
    turned[...] = pltpu.roll(total[...], 64, 1)
    out[:, 0:128] = total[0:20, :]
    out[:, 128:256] = total[20:40, :]
    out[0:10, 256:320] = total[40:50, 0:64]
    out[10:20, 256:320] = turned[40:50, 0:64]


def weight_sums(arrived):
    return pl.pallas_call(
        unpack_kernel,
        out_shape=jax.ShapeDtypeStruct((20, 320), F32),
        in_specs=[whole()],
        out_specs=whole(),
        scratch_shapes=[pltpu.VMEM((56, 128), F32), pltpu.VMEM((56, 128), F32)],
        compiler_params=PARAMS,
    )(arrived)


def on_device(
    llm_grad,
    image_grid,
    image_owner,
    row_start,
    merger_pre,
    vit_out,
    vit_pre,
    ln_gain,
    merger_out_w,
    merger_in_w,
    vit_fc2_w,
):
    x = lax.axis_index("gx")
    core = lax.axis_index("gc")
    own_index = lax.axis_index(SEQ)
    in_w = lax.ppermute(
        merger_in_w.T,
        (*GRP, "z"),
        [
            ((2 * a + c) * 8 + z, (z // 2 * 2 + c) * 8 + 2 * a + z % 2)
            for a in range(4)
            for c in range(2)
            for z in range(8)
        ],
    )

    peers = jnp.arange(64, dtype=jnp.int32)
    my_owners = lax.dynamic_slice_in_dim(image_owner, own_index * 64, 64)
    my_starts = lax.dynamic_slice_in_dim(row_start, own_index * 64, 64)
    my_grids = lax.dynamic_slice_in_dim(image_grid, own_index * 64, 64)
    my_counts = my_grids[:, 0] * my_grids[:, 1]
    targets = (my_owners[None, :] == peers[:, None]).astype(jnp.int32)
    send_counts = jnp.sum(targets * my_counts[None, :], 1)
    send_starts = jnp.sum(targets * my_starts[None, :], 1)
    within = jnp.arange(SLOT, dtype=jnp.int32)
    wanted = jnp.where(
        within[None, :] < send_counts[:, None], send_starts[:, None] + within[None, :], -1
    ).reshape(-1)
    pick = (wanted[:, None] == jnp.arange(llm_grad.shape[0], dtype=jnp.int32)[None, :]).astype(BF16)
    rows = jnp.dot(pick, llm_grad, preferred_element_type=F32).astype(BF16)

    fc2_rows = jnp.pad(vit_fc2_w, ((0, 12), (0, 0)))
    rows, fc2_rows, in_w = lax.optimization_barrier((rows, fc2_rows, in_w))
    table = lax.all_gather(in_w, SEQ, axis=0, tiled=True)
    along_y = lax.all_gather(jnp.concatenate([merger_out_w, fc2_rows], axis=0), "y", axis=0)
    turned = lax.ppermute(
        rows, (*GRP, "z"), [(g * 8 + z, z * 8 + g) for g in range(8) for z in range(8)]
    )
    turned, along_y = lax.optimization_barrier((turned, along_y))
    across = shifted(along_y, "gc", 1)
    top, low = turned[:96], turned[96:]
    left_top = shifted(top, "gx", 1)
    right_low = shifted(low, "gx", -1)
    left_low = shifted(low, "gx", 1)
    right_top = shifted(top, "gx", -1)
    far_top = shifted(left_top, "gx", 1)
    far_low = shifted(right_low, "gx", -1)
    pieces = [top, low, left_top, left_low, right_top, right_low, far_top, far_low]
    order = jnp.stack([(x + step) % 4 for step in (0, 3, 1, 2)]).astype(jnp.int32)
    partial = hidden_products(order, pieces, along_y, across)
    partial, merger_pre, image_owner, image_grid, vit_pre, vit_out = lax.optimization_barrier(
        (partial, merger_pre, image_owner, image_grid, vit_pre, vit_out)
    )
    arrived = lax.all_to_all(partial, SEQ, split_axis=0, concat_axis=0, tiled=True)

    pre_act = merger_pre[:, 0, :].reshape(4, 2, 8, SLOT, -1).transpose(1, 2, 0, 3, 4)
    pre_act = pre_act.reshape(2, 96, -1)
    pre_act = jnp.where(core == 0, pre_act, pre_act[::-1]).reshape(192, -1)
    slope = gelu_slope(pre_act.astype(F32))
    fc2_y = along_y[:, 128:, :].reshape(256, -1)
    arrived, fc2_y = lax.optimization_barrier((arrived, fc2_y))
    fc2 = lax.all_gather(fc2_y, "z", axis=0, tiled=True)
    kept, passed = hidden_sums(arrived)
    hidden = jnp.concatenate([kept, shifted(passed, "gc", 1)], axis=0)
    pre_grad = (slope * hidden.astype(F32)).astype(BF16)
    own, other = merged_products(lax.all_gather(pre_grad, "gx", axis=0), table)
    swapped = shifted(other, "gc", 1)

    grids = image_grid.reshape(64, 64, 2)
    counts = grids[:, :, 0] * grids[:, :, 1]
    widths = grids[:, :, 1]
    owners = image_owner.reshape(64, 64)
    taken = (owners == own_index).astype(jnp.int32)
    recv_counts = jnp.sum(taken * counts, 1)
    recv_widths = jnp.sum(taken * widths, 1)
    j = jnp.arange(SLOT, dtype=jnp.int32)[None, :]
    w = recv_widths[:, None]
    base = peers[:, None] * (4 * SLOT) + (2 * (j // w)) * (2 * w) + 2 * (j % w)
    valid = j < recv_counts[:, None]
    component = jnp.arange(4, dtype=jnp.int32)[:, None, None]
    slots = base[None] + (component // 2) * (2 * w[None]) + component % 2
    slots = jnp.where(valid[None], slots, -1)
    slots = slots.reshape(4, 4, 2, 8, SLOT).transpose(2, 0, 3, 1, 4).reshape(2, 4, 96)
    own_slots = lax.dynamic_index_in_dim(slots, core, 0, keepdims=False)
    other_slots = lax.dynamic_index_in_dim(slots, 1 - core, 0, keepdims=False)
    places = jnp.arange(768, dtype=jnp.int32)
    mine = lax.dynamic_index_in_dim(own_slots, x, 0, keepdims=False)
    take_own = (mine[:, None] == places[None, :]).astype(BF16)
    norm_in = jnp.dot(take_own, vit_out[:, 0, :], preferred_element_type=F32).astype(BF16)
    all_slots = jnp.concatenate([own_slots.reshape(-1), other_slots.reshape(-1)])
    take_all = (all_slots[:, None] == places[None, :]).astype(BF16)
    fc_in = jnp.dot(take_all, vit_pre[:, 0, :], preferred_element_type=F32)
    sigmoid_q = jax.nn.sigmoid(1.702 * fc_in)
    activation = (fc_in * sigmoid_q).astype(BF16)
    fc_slope = sigmoid_q + 1.702 * fc_in * sigmoid_q * (1.0 - sigmoid_q)

    grad = norm_backward(own, swapped, norm_in, ln_gain.reshape(1, -1))
    near_grad = lax.all_gather(grad, "gx", axis=0, tiled=True)
    far_grad = shifted(near_grad, "gc", 1)
    sent = weight_products(near_grad, far_grad, activation)
    weight_grad = weight_sums(
        lax.all_to_all(sent, SEQ, split_axis=0, concat_axis=0, tiled=True)
    )

    grads = jnp.concatenate([near_grad, far_grad], axis=0)
    fc2 = fc2.reshape(64, 32, -1)[:, :20].reshape(1280, -1)
    act_grad = jnp.dot(grads, fc2, preferred_element_type=F32)
    fc1_rows = (fc_slope * act_grad).astype(BF16)
    fc1_grad = jnp.dot(take_all.T, fc1_rows, preferred_element_type=F32).astype(BF16)
    g = lax.axis_index(GRP)
    own_places = g * 96 + jnp.arange(96, dtype=jnp.int32)
    put_own = (own_places[:, None] == all_slots[None, :]).astype(BF16)
    own_rows = jnp.dot(put_own, grads, preferred_element_type=F32).astype(BF16)
    return (
        own_rows.reshape(96, 1, -1),
        fc1_grad.reshape(768, 1, -1),
        weight_grad,
    )


def solution(mesh):
    finer = Mesh(mesh.devices.reshape(4, 2, 8, 8), ("gx", "gc", "z", "y"))
    in_specs = (
        P(SEQ, GRP),
        P(),
        P(),
        P(),
        P(None, SEQ, GRP),
        P(None, SEQ, None),
        P(None, SEQ, GRP),
        P(),
        P(SEQ, GRP),
        P(GRP, SEQ),
        P(SEQ, GRP),
    )
    out_specs = (P(GRP, SEQ, None), P(None, SEQ, GRP), P(SEQ, GRP))
    return jax.shard_map(
        on_device, mesh=finer, in_specs=in_specs, out_specs=out_specs, check_vma=False
    )
```

```python
import jax
import jax.numpy as jnp
from jax import lax
from jax.experimental import pallas as pl
from jax.experimental.pallas import tpu as pltpu
from jax.sharding import Mesh
from jax.sharding import PartitionSpec as P

SLOT = 3
SEQ = ("z", "y")
GRP = ("gx", "gc")
BF16 = jnp.bfloat16
F32 = jnp.float32
PARAMS = pltpu.CompilerParams(vmem_limit_bytes=48 * 1024 * 1024)


def whole(memory=pltpu.VMEM):
    return pl.BlockSpec(memory_space=memory)


def shifted(value, axis, step):
    size = lax.axis_size(axis)
    return lax.ppermute(value, axis, [(i, (i + step) % size) for i in range(size)])


def gelu_slope(values):
    return (
        0.5 * (1.0 + lax.erf(values * 0.7071067811865476))
        + values * jnp.exp(-0.5 * values * values) * 0.3989422804014327
    )


def hidden_kernel(order, *refs):
    pieces, (near, far, out, sums, table) = refs[:8], refs[8:]
    table[:, 256:384] = jnp.zeros((1024, 128), BF16)
    for core, weight in enumerate((near, far)):
        for k in range(8):
            table[k * 128 : (k + 1) * 128, 0:320] = weight[k, 0:128, :]
        w = table[...]
        for place in range(4):
            rows = jnp.concatenate([half[...] for half in pieces[2 * place : 2 * place + 2]], axis=0)
            sums[order[place] + 4 * core] = jnp.dot(rows, w, preferred_element_type=F32)
    row = lax.broadcasted_iota(jnp.int32, (192, 192), 0)
    col = lax.broadcasted_iota(jnp.int32, (192, 192), 1)
    wanted = (row // 3 % 8) * 24 + (row // 24) * 3 + row % 3
    turn = jnp.where(wanted == col, 1.0, 0.0).astype(BF16)
    for part in range(8):
        block = sums[:, part * 24 : (part + 1) * 24, :].reshape(192, -1).astype(BF16)
        turned = jnp.dot(turn, block, preferred_element_type=F32)
        last = turned[:, 256:384]
        shifted_last = pltpu.roll(last, 64, 1).reshape(8, 24, 128)
        last = last.reshape(8, 24, 128)
        packed = jnp.concatenate(
            [
                turned[:, 0:128].reshape(8, 24, 128),
                turned[:, 128:256].reshape(8, 24, 128),
                last[:, 0:8] + shifted_last[:, 8:16],
                last[:, 16:24],
            ],
            axis=1,
        )
        out[part * 8 : (part + 1) * 8] = packed.astype(BF16)


def hidden_products(order, pieces, near, far):
    return pl.pallas_call(
        hidden_kernel,
        out_shape=jax.ShapeDtypeStruct((64, 64, 128), BF16),
        in_specs=[whole(pltpu.SMEM)] + [whole()] * 10,
        out_specs=whole(),
        scratch_shapes=[pltpu.VMEM((8, 192, 384), F32), pltpu.VMEM((1024, 384), BF16)],
        compiler_params=PARAMS,
    )(order, *pieces, near, far)


def sum_kernel(arrived, keep, send):
    total = arrived[0:8].astype(F32)
    for k in range(1, 8):
        total = total + arrived[8 * k : 8 * k + 8].astype(F32)
    last = total[:, 48:56]
    second = pltpu.roll(last.reshape(64, 128), 64, 1).reshape(8, 8, 128)
    last = jnp.concatenate([last, second, total[:, 56:64]], axis=1)
    hidden = jnp.concatenate(
        [part.reshape(192, 128) for part in (total[:, 0:24], total[:, 24:48], last)], axis=1
    ).astype(BF16)
    row = lax.broadcasted_iota(jnp.int32, (96, 192), 0)
    col = lax.broadcasted_iota(jnp.int32, (96, 192), 1)
    first = row // 12 * 24 + row % 12
    for half, out in enumerate((keep, send)):
        pick = jnp.where(first + 12 * half == col, 1.0, 0.0).astype(BF16)
        out[...] = jnp.dot(pick, hidden, preferred_element_type=F32)[:, 0:320].astype(BF16)


def hidden_sums(arrived):
    half = jax.ShapeDtypeStruct((96, 320), BF16)
    return pl.pallas_call(
        sum_kernel,
        out_shape=(half, half),
        in_specs=[whole()],
        out_specs=(whole(), whole()),
        compiler_params=PARAMS,
    )(arrived)


def merged_kernel(grads, table, own, other):
    dims = (((1,), (1,)), ((), ()))
    total = None
    for k in range(4):
        w = table[k * 1280 : (k + 1) * 1280, :]
        part = lax.dot_general(grads[k], w, dims, preferred_element_type=F32)
        total = part if total is None else total + part
    own[...] = total[:96]
    other[...] = total[96:].astype(BF16)


def merged_products(grads, table):
    return pl.pallas_call(
        merged_kernel,
        out_shape=(
            jax.ShapeDtypeStruct((96, 1280), F32),
            jax.ShapeDtypeStruct((96, 1280), BF16),
        ),
        in_specs=[whole()] * 2,
        out_specs=(whole(), whole()),
        compiler_params=PARAMS,
    )(grads, table)


def norm_kernel(own, swapped, inputs, gain, out):
    upstream = own[...] + swapped[...].astype(F32)
    x = inputs[...].astype(F32)
    centred = x - jnp.mean(x, -1, keepdims=True)
    inverse_std = lax.rsqrt(jnp.mean(centred * centred, -1, keepdims=True) + 1e-06)
    normed = centred * inverse_std
    scaled = upstream * gain[...]
    out[...] = (
        inverse_std
        * (
            scaled
            - jnp.mean(scaled, -1, keepdims=True)
            - normed * jnp.mean(scaled * normed, -1, keepdims=True)
        )
    ).astype(BF16)


def norm_backward(own, swapped, inputs, gain):
    return pl.pallas_call(
        norm_kernel,
        out_shape=jax.ShapeDtypeStruct((96, 1280), BF16),
        in_specs=[whole()] * 4,
        out_specs=whole(),
        compiler_params=PARAMS,
    )(own, swapped, inputs, gain)


def weight_kernel(near, far, activation, out, total, turned, packed):
    dims = (((0,), (0,)), ((), ()))
    total[:, 256:384] = jnp.zeros((1280, 128), F32)
    total[:, 0:320] = lax.dot_general(
        near[...], activation[0:384, :], dims, preferred_element_type=F32
    ) + lax.dot_general(far[...], activation[384:768, :], dims, preferred_element_type=F32)
    turned[...] = pltpu.roll(total[:, 256:384], 64, 1)
    for s in range(64):
        row = s * 20
        packed[s, 0:20, :] = total[row : row + 20, 0:128]
        packed[s, 20:40, :] = total[row : row + 20, 128:256]
        packed[s, 40:50, :] = total[row : row + 10, 256:384] + turned[row + 10 : row + 20, :]
        packed[s, 50:56, :] = jnp.zeros((6, 128), F32)
    out[...] = packed[...].astype(BF16)


def weight_products(near, far, activation):
    return pl.pallas_call(
        weight_kernel,
        out_shape=jax.ShapeDtypeStruct((64, 56, 128), BF16),
        in_specs=[whole()] * 3,
        out_specs=whole(),
        scratch_shapes=[
            pltpu.VMEM((1280, 384), F32),
            pltpu.VMEM((1280, 128), F32),
            pltpu.VMEM((64, 56, 128), F32),
        ],
        compiler_params=PARAMS,
    )(near, far, activation)


def unpack_kernel(arrived, out, total, turned):
    total[...] = jnp.sum(arrived[...].astype(F32), axis=0)
    turned[...] = pltpu.roll(total[...], 64, 1)
    out[:, 0:128] = total[0:20, :]
    out[:, 128:256] = total[20:40, :]
    out[0:10, 256:320] = total[40:50, 0:64]
    out[10:20, 256:320] = turned[40:50, 0:64]


def weight_sums(arrived):
    return pl.pallas_call(
        unpack_kernel,
        out_shape=jax.ShapeDtypeStruct((20, 320), F32),
        in_specs=[whole()],
        out_specs=whole(),
        scratch_shapes=[pltpu.VMEM((56, 128), F32), pltpu.VMEM((56, 128), F32)],
        compiler_params=PARAMS,
    )(arrived)


def on_device(
    llm_grad,
    image_grid,
    image_owner,
    row_start,
    merger_pre,
    vit_out,
    vit_pre,
    ln_gain,
    merger_out_w,
    merger_in_w,
    vit_fc2_w,
):
    x = lax.axis_index("gx")
    core = lax.axis_index("gc")
    own_index = lax.axis_index(SEQ)
    in_w = lax.ppermute(
        merger_in_w.T,
        (*GRP, "z"),
        [
            ((2 * a + c) * 8 + z, (z // 2 * 2 + c) * 8 + 2 * a + z % 2)
            for a in range(4)
            for c in range(2)
            for z in range(8)
        ],
    )

    peers = jnp.arange(64, dtype=jnp.int32)
    my_owners = lax.dynamic_slice_in_dim(image_owner, own_index * 64, 64)
    my_starts = lax.dynamic_slice_in_dim(row_start, own_index * 64, 64)
    my_grids = lax.dynamic_slice_in_dim(image_grid, own_index * 64, 64)
    my_counts = my_grids[:, 0] * my_grids[:, 1]
    targets = (my_owners[None, :] == peers[:, None]).astype(jnp.int32)
    send_counts = jnp.sum(targets * my_counts[None, :], 1)
    send_starts = jnp.sum(targets * my_starts[None, :], 1)
    within = jnp.arange(SLOT, dtype=jnp.int32)
    wanted = jnp.where(
        within[None, :] < send_counts[:, None], send_starts[:, None] + within[None, :], -1
    ).reshape(-1)
    pick = (wanted[:, None] == jnp.arange(llm_grad.shape[0], dtype=jnp.int32)[None, :]).astype(BF16)
    rows = jnp.dot(pick, llm_grad, preferred_element_type=F32).astype(BF16)

    rows, vit_fc2_w, in_w = lax.optimization_barrier((rows, vit_fc2_w, in_w))
    table = lax.all_gather(in_w, SEQ, axis=0, tiled=True)
    along_y = lax.all_gather(jnp.pad(jnp.concatenate([merger_out_w, vit_fc2_w], axis=0), ((0, 12), (0, 0))), "y", axis=0)
    turned = lax.ppermute(
        rows, (*GRP, "z"), [(g * 8 + z, z * 8 + g) for g in range(8) for z in range(8)]
    )
    turned, along_y = lax.optimization_barrier((turned, along_y))
    across = shifted(along_y, "gc", 1)
    top, low = turned[:96], turned[96:]
    left_top = shifted(top, "gx", 1)
    right_low = shifted(low, "gx", -1)
    left_low = shifted(low, "gx", 1)
    right_top = shifted(top, "gx", -1)
    far_top = shifted(left_top, "gx", 1)
    far_low = shifted(right_low, "gx", -1)
    pieces = [top, low, left_top, left_low, right_top, right_low, far_top, far_low]
    order = jnp.stack([(x + step) % 4 for step in (0, 3, 1, 2)]).astype(jnp.int32)
    partial = hidden_products(order, pieces, along_y, across)
    partial, merger_pre, image_owner, image_grid, vit_pre, vit_out = lax.optimization_barrier(
        (partial, merger_pre, image_owner, image_grid, vit_pre, vit_out)
    )
    arrived = lax.all_to_all(partial, SEQ, split_axis=0, concat_axis=0, tiled=True)

    pre_act = merger_pre[:, 0, :].reshape(4, 2, 8, SLOT, -1).transpose(1, 2, 0, 3, 4)
    pre_act = pre_act.reshape(2, 96, -1)
    pre_act = jnp.where(core == 0, pre_act, pre_act[::-1]).reshape(192, -1)
    slope = gelu_slope(pre_act.astype(F32))
    fc2_y = along_y[:, 128:, :].reshape(256, -1)
    arrived, fc2_y = lax.optimization_barrier((arrived, fc2_y))
    fc2 = lax.all_gather(fc2_y, "z", axis=0, tiled=True)
    kept, passed = hidden_sums(arrived)
    hidden = jnp.concatenate([kept, shifted(passed, "gc", 1)], axis=0)
    pre_grad = (slope * hidden.astype(F32)).astype(BF16)
    own, other = merged_products(lax.all_gather(pre_grad, "gx", axis=0), table)
    swapped = shifted(other, "gc", 1)

    grids = image_grid.reshape(64, 64, 2)
    counts = grids[:, :, 0] * grids[:, :, 1]
    widths = grids[:, :, 1]
    owners = image_owner.reshape(64, 64)
    taken = (owners == own_index).astype(jnp.int32)
    recv_counts = jnp.sum(taken * counts, 1)
    recv_widths = jnp.sum(taken * widths, 1)
    j = jnp.arange(SLOT, dtype=jnp.int32)[None, :]
    w = recv_widths[:, None]
    base = peers[:, None] * (4 * SLOT) + (2 * (j // w)) * (2 * w) + 2 * (j % w)
    valid = j < recv_counts[:, None]
    component = jnp.arange(4, dtype=jnp.int32)[:, None, None]
    slots = base[None] + (component // 2) * (2 * w[None]) + component % 2
    slots = jnp.where(valid[None], slots, -1)
    slots = slots.reshape(4, 4, 2, 8, SLOT).transpose(2, 0, 3, 1, 4).reshape(2, 4, 96)
    own_slots = lax.dynamic_index_in_dim(slots, core, 0, keepdims=False)
    other_slots = lax.dynamic_index_in_dim(slots, 1 - core, 0, keepdims=False)
    places = jnp.arange(768, dtype=jnp.int32)
    mine = lax.dynamic_index_in_dim(own_slots, x, 0, keepdims=False)
    take_own = (mine[:, None] == places[None, :]).astype(BF16)
    norm_in = jnp.dot(take_own, vit_out[:, 0, :], preferred_element_type=F32).astype(BF16)
    all_slots = jnp.concatenate([own_slots.reshape(-1), other_slots.reshape(-1)])
    take_all = (all_slots[:, None] == places[None, :]).astype(BF16)
    fc_in = jnp.dot(take_all, vit_pre[:, 0, :], preferred_element_type=F32)
    sigmoid_q = jax.nn.sigmoid(1.702 * fc_in)
    activation = (fc_in * sigmoid_q).astype(BF16)
    fc_slope = sigmoid_q + 1.702 * fc_in * sigmoid_q * (1.0 - sigmoid_q)

    grad = norm_backward(own, swapped, norm_in, ln_gain.reshape(1, -1))
    near_grad = lax.all_gather(grad, "gx", axis=0, tiled=True)
    far_grad = shifted(near_grad, "gc", 1)
    sent = weight_products(near_grad, far_grad, activation)
    weight_grad = weight_sums(
        lax.all_to_all(sent, SEQ, split_axis=0, concat_axis=0, tiled=True)
    )

    grads = jnp.concatenate([near_grad, far_grad], axis=0)
    fc2 = fc2.reshape(64, 32, -1)[:, :20].reshape(1280, -1)
    act_grad = jnp.dot(grads, fc2, preferred_element_type=F32)
    fc1_rows = (fc_slope * act_grad).astype(BF16)
    fc1_grad = jnp.dot(take_all.T, fc1_rows, preferred_element_type=F32).astype(BF16)
    g = lax.axis_index(GRP)
    own_places = g * 96 + jnp.arange(96, dtype=jnp.int32)
    put_own = (own_places[:, None] == all_slots[None, :]).astype(BF16)
    own_rows = jnp.dot(put_own, grads, preferred_element_type=F32).astype(BF16)
    return (
        own_rows.reshape(96, 1, -1),
        fc1_grad.reshape(768, 1, -1),
        weight_grad,
    )


def solution(mesh):
    finer = Mesh(mesh.devices.reshape(4, 2, 8, 8), ("gx", "gc", "z", "y"))
    in_specs = (
        P(SEQ, GRP),
        P(),
        P(),
        P(),
        P(None, SEQ, GRP),
        P(None, SEQ, None),
        P(None, SEQ, GRP),
        P(),
        P(SEQ, GRP),
        P(GRP, SEQ),
        P(SEQ, GRP),
    )
    out_specs = (P(GRP, SEQ, None), P(None, SEQ, GRP), P(SEQ, GRP))
    return jax.shard_map(
        on_device, mesh=finer, in_specs=in_specs, out_specs=out_specs, check_vma=False
    )
```
